32 devices in a mesh: tm: 8 (over y, x, core), mp: 4 (over z).
Axes of the slice: x: 2, y: 2, z: 4, core: 2. Of those that a mesh axis runs over, the one named last changes fastest.
Arguments:
- states: bfloat16 [16, 384, 3072], P('tm', None, 'mp'), may hold values from -6 to 6
- key_cache: bfloat16 [64, 384, 3072], P('tm', None, 'mp'), may hold values from -6 to 6
- value_cache: bfloat16 [64, 384, 3072], P('tm', None, 'mp'), may hold values from -6 to 6
- frame_times: int32 [16], replicated, may hold values from 0 to 15, each once
- valid_counts: int32 [384], P('tm'), may hold values from 1 to 64, as said below
- qkv_weight: bfloat16 [3072, 3, 3072], P(None, None, 'mp'), may hold values from -0.109375 to 0.109375
- out_weight: bfloat16 [3072, 3072], P('mp'), may hold values from -0.5 to 0.5
- up_weight: bfloat16 [3072, 6144], P(None, 'mp'), may hold values from -0.109375 to 0.109375
- down_weight: bfloat16 [6144, 3072], P('mp'), may hold values from -0.078125 to 0.078125
Outputs:
- next_states: bfloat16 [16, 384, 3072], P('tm', None, 'mp')
The draws below stay inside these ranges and needn't reach their ends.
Inputs may be any that keep to these rules, and one draw needn't show every extreme that they name: `frame_times`: every new frame has a different time index. `valid_counts`: some patch may attend to all 64 cached frames and some to one.
All inputs are finite; a program needn't handle non-finite values.
Results may differ from the reference program's by a relative error of at most 0.015.
Values may be sent and summed in bfloat16 or wider, within the bound.
A program may use at most 192 MiB of HBM per device.

```python
import math
import jax
import jax.numpy as jnp
from jax import lax

D = 3072
HEADS = 24
HD = 128
FF = 6144
P_SIZE = 384
FRAMES = 16
CACHE = 64
N_MP = 4


def draw_valid_counts(key, part):
    key = jax.random.fold_in(key, 11)
    first, second = jax.random.split(key)
    counts = jax.random.randint(first, (P_SIZE,), 1, CACHE + 1, dtype=jnp.int32)
    chosen = jax.random.randint(second, (), 0, P_SIZE, dtype=jnp.int32)
    counts = counts.at[chosen].set(CACHE)
    counts = counts.at[(chosen + 1) % P_SIZE].set(1)
    return counts


def shard_levels(key, shape, shards, low, high):
    loudness = 1.0
    for axis_at, parts in shards:
        heights = jax.random.uniform(jax.random.fold_in(jax.random.fold_in(key, 6), axis_at), (parts,), jnp.float32, low / len(shards), high / len(shards))
        loudness = loudness * jnp.repeat(jnp.exp(heights), shape[axis_at] // parts).reshape((-1,) + (1,) * (len(shape) - 1 - axis_at))
    return loudness


def centred(rng, extent, width, reach, pieces=(), kind=jnp.bfloat16):
    values = width * jax.random.normal(rng, extent, jnp.float32)
    if pieces:
        values = values * shard_levels(rng, extent, pieces, -0.22, 0.18)
    return jnp.clip(values, -reach, reach).astype(kind)


def setup_inputs(seed: int = 0) -> dict:
    seeds = jax.random.split(jax.random.key(seed), 10)
    return {
        "states": centred(seeds[0], (FRAMES, P_SIZE, D), 1.0, 6.0, ((0, 8), (2, 4))),
        "key_cache": centred(seeds[1], (CACHE, P_SIZE, D), 1.0, 6.0, ((0, 8), (2, 4))),
        "value_cache": centred(seeds[2], (CACHE, P_SIZE, D), 1.0, 6.0, ((0, 8), (2, 4))),
        "frame_times": jax.random.permutation(seeds[3], FRAMES).astype(jnp.int32),
        "valid_counts": draw_valid_counts(jax.random.fold_in(seeds[9], 71), 0),
        "qkv_weight": centred(seeds[5], (D, 3, D), D ** -0.5, 0.109375, ((2, 4),)),
        "out_weight": centred(seeds[6], (D, D), HD ** -0.5, 0.5, ((0, 4),)),
        "up_weight": centred(seeds[7], (D, FF), D ** -0.5, 0.109375, ((1, 4),)),
        "down_weight": centred(seeds[8], (FF, D), FF ** -0.5, 0.078125, ((0, 4),)),
    }


def row_norm(values):
    widened = values.astype(jnp.float32)
    mean_square = lax.optimization_barrier(jnp.mean(widened * widened, axis=-1, keepdims=True))
    return (widened * lax.rsqrt(mean_square + 1e-06)).astype(jnp.bfloat16)

def grouped(left, right, groups):
    span = left.shape[1] // groups
    total = jnp.zeros((left.shape[0], right.shape[1]), jnp.float32)
    for group in range(groups):
        term = jnp.dot(left[:, group * span:(group + 1) * span], right[group * span:(group + 1) * span], preferred_element_type=jnp.float32)
        term = lax.optimization_barrier(term.astype(jnp.bfloat16)).astype(jnp.float32)
        total = total + term
    return total

def reference(states, key_cache, value_cache, frame_times, valid_counts, qkv_weight, out_weight, up_weight, down_weight):
    token_rows = states.reshape(FRAMES * P_SIZE, D)
    normed = row_norm(token_rows)
    projected = jnp.dot(normed, qkv_weight.reshape(D, 3 * D), preferred_element_type=jnp.float32)
    projected = projected.astype(jnp.bfloat16).reshape(FRAMES, P_SIZE, 3, HEADS, HD)
    queries = row_norm(projected[:, :, 0])
    fresh_keys = row_norm(projected[:, :, 1])
    fresh_values = projected[:, :, 2]
    cached_keys = row_norm(key_cache.reshape(CACHE, P_SIZE, HEADS, HD))
    cached_values = value_cache.reshape(CACHE, P_SIZE, HEADS, HD)
    all_keys = jnp.concatenate([cached_keys, fresh_keys], axis=0)
    all_values = jnp.concatenate([cached_values, fresh_values], axis=0)
    cached_ok = jnp.arange(CACHE, dtype=jnp.int32)[None, :] >= (CACHE - valid_counts)[:, None]
    fresh_ok = frame_times[None, :] <= frame_times[:, None]
    allowed = jnp.concatenate([jnp.broadcast_to(cached_ok[:, None, :], (P_SIZE, FRAMES, CACHE)), jnp.broadcast_to(fresh_ok[None], (P_SIZE, FRAMES, FRAMES))], axis=-1)
    scale = 1.0 / math.sqrt(HD)

    def one_head(items):
        query_head, key_head, value_head = items
        scores = jnp.einsum('fpe,kpe->pfk', query_head.astype(jnp.float32), key_head.astype(jnp.float32)) * scale
        raised = jnp.where(allowed, jnp.exp(scores), 0.0)
        attn_weights = (raised / lax.optimization_barrier(jnp.sum(raised, axis=-1, keepdims=True))).astype(jnp.bfloat16)
        mixed = jnp.einsum('pfk,kpe->fpe', attn_weights.astype(jnp.float32), value_head.astype(jnp.float32))
        return mixed.astype(jnp.bfloat16)
    heads_out = lax.map(one_head, (jnp.moveaxis(queries, 2, 0), jnp.moveaxis(all_keys, 2, 0), jnp.moveaxis(all_values, 2, 0)))
    heads_rows = jnp.moveaxis(heads_out, 0, 2).reshape(FRAMES * P_SIZE, D)
    attn_sum = grouped(heads_rows, out_weight, N_MP)
    mid = (token_rows.astype(jnp.float32) + attn_sum).astype(jnp.bfloat16)
    hidden = jax.nn.gelu(jnp.dot(row_norm(mid), up_weight, preferred_element_type=jnp.float32)).astype(jnp.bfloat16)
    next_states = (mid.astype(jnp.float32) + grouped(hidden, down_weight, N_MP)).astype(jnp.bfloat16)
    return next_states.reshape(FRAMES, P_SIZE, D)
```

```python
import functools
import math

import jax
import jax.numpy as jnp
from jax import lax
from jax.experimental import pallas as pl
from jax.experimental.pallas import tpu as pltpu
from jax.sharding import PartitionSpec as P

HD = 128
MESH = pl.DeviceIdType.MESH
CHUNKS = 8


def unit_rows(tensor):
    widened = tensor.astype(jnp.float32)
    mean_square = jnp.mean(widened * widened, axis=-1, keepdims=True)
    return (widened * lax.rsqrt(mean_square + 1e-06)).astype(jnp.bfloat16)


def attend_kernel(patches, counts_ref, mask_ref, fresh_ref, keys_ref, values_ref, out_ref):
    devices, _, share, width = keys_ref.shape
    frames = fresh_ref.shape[1]
    cache = devices * share
    heads = width // HD
    scale = 1.0 / math.sqrt(HD)
    fresh_ok = mask_ref[...] > 0.5
    lane = lax.broadcasted_iota(jnp.int32, mask_ref.shape, 1)
    for p in range(patches):
        count = counts_ref[pl.program_id(0) * patches + p]
        allowed = ((lane >= cache - count) & (lane < cache)) | fresh_ok
        fresh = fresh_ref[p].astype(jnp.float32)
        old_keys = keys_ref[:, p].astype(jnp.float32).reshape(cache, width)
        old_values = values_ref[:, p].astype(jnp.float32).reshape(cache, width)
        all_keys = jnp.concatenate([old_keys, fresh[:, width : 2 * width]], axis=0)
        all_values = jnp.concatenate([old_values, fresh[:, 2 * width :]], axis=0).astype(jnp.bfloat16)
        scores = []
        for h in range(heads):
            at = slice(h * HD, (h + 1) * HD)
            scores.append(
                lax.dot_general(
                    unit_rows(fresh[:, at]),
                    unit_rows(all_keys[:, at]),
                    (((1,), (1,)), ((), ())),
                    preferred_element_type=jnp.float32,
                )
            )
        raised = jnp.where(allowed, jnp.exp(jnp.concatenate(scores, axis=0) * scale), 0.0)
        weights = (raised / jnp.sum(raised, axis=-1, keepdims=True)).astype(jnp.bfloat16)
        for h in range(heads):
            at = slice(h * HD, (h + 1) * HD)
            out_ref[p, :, at] = jnp.dot(
                weights[h * frames : (h + 1) * frames], all_values[:, at], preferred_element_type=jnp.float32
            ).astype(jnp.bfloat16)


def attend(fresh, cached_keys, cached_values, frame_times, valid_counts):
    patch_count, frames, _ = fresh.shape
    devices, _, share, width = cached_keys.shape
    cache = devices * share
    heads = width // HD
    patches = 4
    fresh_ok = (frame_times[None, :] <= frame_times[:, None]).astype(jnp.float32)
    mask = jnp.concatenate([jnp.zeros((frames, cache), jnp.float32), fresh_ok], axis=1)
    mask = jnp.tile(mask, (heads, 1))
    cache_spec = pl.BlockSpec((devices, patches, share, width), lambda s: (0, s, 0, 0))
    return pl.pallas_call(
        functools.partial(attend_kernel, patches),
        grid=(patch_count // patches,),
        in_specs=[
            pl.BlockSpec(memory_space=pltpu.SMEM),
            pl.BlockSpec(mask.shape, lambda s: (0, 0)),
            pl.BlockSpec((patches, frames, 3 * width), lambda s: (s, 0, 0)),
            cache_spec,
            cache_spec,
        ],
        out_specs=pl.BlockSpec((patches, frames, width), lambda s: (s, 0, 0)),
        out_shape=jax.ShapeDtypeStruct((patch_count, frames, width), jnp.bfloat16),
        compiler_params=pltpu.CompilerParams(vmem_limit_bytes=40 * 2**20),
        name="attend",
    )(valid_counts, mask, fresh, cached_keys, cached_values)


def tail_kernel(
    n, chunks,
    heads_ref, states_ref, out_w_hbm, up_w_hbm, down_w_hbm, result_ref,
    out_w, up_w, down_w, terms, landed, middle,
    weight_sem, sum_send, sum_recv, right_send, left_send, gather_recv,
):
    me = lax.axis_index("mp")
    rows, width = states_ref.shape[1:]
    last = n - 1

    loads = [
        pltpu.make_async_copy(src, dst, weight_sem.at[k])
        for k, (src, dst) in enumerate(((out_w_hbm, out_w), (up_w_hbm, up_w), (down_w_hbm, down_w)))
    ]
    for load in loads:
        load.start()

    barrier = pltpu.get_barrier_semaphore()

    @pl.when(me > 0)
    def _():
        pl.semaphore_signal(barrier, inc=1, device_id={"mp": me - 1}, device_id_type=MESH)

    @pl.when(me < last)
    def _():
        pl.semaphore_signal(barrier, inc=1, device_id={"mp": me + 1}, device_id_type=MESH)

    @pl.when((me > 0) & (me < last))
    def _():
        pl.semaphore_wait(barrier, 2)

    @pl.when((me == 0) | (me == last))
    def _():
        pl.semaphore_wait(barrier, 1)

    def sum_copy(c, d, slot, target):
        return pltpu.make_async_remote_copy(
            src_ref=terms.at[c, d],
            dst_ref=landed.at[c, slot],
            send_sem=sum_send.at[c, d],
            recv_sem=sum_recv.at[c, slot],
            device_id={"mp": target},
            device_id_type=MESH,
        )

    def gather_copy(c, d, send_sem, target):
        return pltpu.make_async_remote_copy(
            src_ref=middle.at[c, d],
            dst_ref=middle.at[c, d],
            send_sem=send_sem.at[c, d],
            recv_sem=gather_recv.at[c, d],
            device_id={"mp": target},
            device_id_type=MESH,
        )

    def active(c):
        return (c >= 0) & (c < chunks)

    def add_landed(c, d, slot):
        sum_copy(c, d, slot, me).wait_recv()
        terms[c, d] = (
            terms[c, d].astype(jnp.float32) + landed[c, slot].astype(jnp.float32)
        ).astype(jnp.bfloat16)

    def sum_right(tick):
        c = tick - me
        for d in range(last, 0, -1):
            @pl.when(active(c) & (me < d))
            def _():
                @pl.when(me > 0)
                def _():
                    add_landed(c, d, d)

                sum_copy(c, d, d, me + 1).start()

    def sum_left(tick):
        c = tick - (last - me)
        for d in range(last):
            @pl.when(active(c) & (me > d))
            def _():
                @pl.when(me < last)
                def _():
                    add_landed(c, d, d)

                @pl.when(me - 1 == d)
                def _():
                    sum_copy(c, d, n, me - 1).start()

                @pl.when(me - 1 > d)
                def _():
                    sum_copy(c, d, d, me - 1).start()

    def sum_end(c):
        @pl.when(me > 0)
        def _():
            sum_copy(c, me, me, me).wait_recv()

        @pl.when(me < last)
        def _():
            sum_copy(c, me, n, me).wait_recv()

        zero = jnp.zeros((rows, width), jnp.float32)
        from_left = jnp.where(me > 0, landed[c, me].astype(jnp.float32), zero)
        from_right = jnp.where(me < last, landed[c, n].astype(jnp.float32), zero)
        return terms[c, me].astype(jnp.float32) + from_left + from_right

    def wait_sum_sends(c):
        for d in range(n):
            @pl.when(me != d)
            def _():
                sum_copy(c, d, d, me).wait_send()

    def step(tick, carry):
        base = tick - 2 * last


        for h in range(last, 0, -1):
            c = tick - last - h

            @pl.when(active(c) & (me - h >= 0))
            def _():
                gather_copy(c, me - h, right_send, me).wait_recv()

                @pl.when(me < last)
                def _():
                    gather_copy(c, me - h, right_send, me + 1).start()

            @pl.when(active(c) & (me + h <= last))
            def _():
                gather_copy(c, me + h, left_send, me).wait_recv()

                @pl.when(me > 0)
                def _():
                    gather_copy(c, me + h, left_send, me - 1).start()

        @pl.when(tick < chunks)
        def _():
            block = heads_ref[tick]
            for d in range(n):
                terms[tick, d] = jnp.dot(
                    block, out_w[:, d * width : (d + 1) * width], preferred_element_type=jnp.float32
                ).astype(jnp.bfloat16)

        sum_right(tick)
        sum_left(tick)

        c_mid = tick - last

        @pl.when(active(c_mid))
        def _():
            total = sum_end(c_mid)
            middle[c_mid, me] = (states_ref[c_mid].astype(jnp.float32) + total).astype(jnp.bfloat16)

            @pl.when(me < last)
            def _():
                gather_copy(c_mid, me, right_send, me + 1).start()

            @pl.when(me > 0)
            def _():
                gather_copy(c_mid, me, left_send, me - 1).start()

        @pl.when(active(base))
        def _():
            wait_sum_sends(base)
            squares = jnp.zeros((rows, 1), jnp.float32)
            for d in range(n):
                block = middle[base, d].astype(jnp.float32)
                squares = squares + jnp.sum(block * block, axis=-1, keepdims=True)
            factor = lax.rsqrt(squares / (n * width) + 1e-06)
            hidden = None
            for d in range(n):
                normed = (middle[base, d].astype(jnp.float32) * factor).astype(jnp.bfloat16)
                part = jnp.dot(
                    normed, up_w[d * width : (d + 1) * width, :], preferred_element_type=jnp.float32
                )
                hidden = part if hidden is None else hidden + part
            hidden = jax.nn.gelu(hidden).astype(jnp.bfloat16)
            for d in range(n):
                terms[base, d] = jnp.dot(
                    hidden, down_w[:, d * width : (d + 1) * width], preferred_element_type=jnp.float32
                ).astype(jnp.bfloat16)

        sum_right(base)
        sum_left(base)

        c_end = base - last

        @pl.when(active(c_end))
        def _():
            total = sum_end(c_end)
            result_ref[c_end] = (middle[c_end, me].astype(jnp.float32) + total).astype(jnp.bfloat16)

        return carry

    loads[0].wait()
    lax.fori_loop(0, 2 * last, step, 0)
    loads[1].wait()
    loads[2].wait()
    lax.fori_loop(2 * last, chunks + 3 * last, step, 0)

    def drain(c, carry):
        wait_sum_sends(c)
        for d in range(n):
            @pl.when((d <= me) & (me < last))
            def _():
                gather_copy(c, d, right_send, me).wait_send()

            @pl.when((d >= me) & (me > 0))
            def _():
                gather_copy(c, d, left_send, me).wait_send()
        return carry

    lax.fori_loop(0, chunks, drain, 0)


def tail(n, states, heads_rows, out_weight, up_weight, down_weight):
    count, width = states.shape
    rows = count // CHUNKS
    states = states.reshape(CHUNKS, rows, width)
    heads_rows = heads_rows.reshape(CHUNKS, rows, width)
    vmem = pl.BlockSpec(memory_space=pltpu.VMEM)
    hbm = pl.BlockSpec(memory_space=pl.ANY)
    result = pl.pallas_call(
        functools.partial(tail_kernel, n, CHUNKS),
        out_shape=jax.ShapeDtypeStruct(states.shape, jnp.bfloat16),
        in_specs=[vmem, vmem, hbm, hbm, hbm],
        out_specs=vmem,
        scratch_shapes=[
            pltpu.VMEM(out_weight.shape, jnp.bfloat16),
            pltpu.VMEM(up_weight.shape, jnp.bfloat16),
            pltpu.VMEM(down_weight.shape, jnp.bfloat16),
            pltpu.VMEM((CHUNKS, n, rows, width), jnp.bfloat16),
            pltpu.VMEM((CHUNKS, n + 1, rows, width), jnp.bfloat16),
            pltpu.VMEM((CHUNKS, n, rows, width), jnp.bfloat16),
            pltpu.SemaphoreType.DMA((3,)),
            pltpu.SemaphoreType.DMA((CHUNKS, n)),
            pltpu.SemaphoreType.DMA((CHUNKS, n + 1)),
            pltpu.SemaphoreType.DMA((CHUNKS, n)),
            pltpu.SemaphoreType.DMA((CHUNKS, n)),
            pltpu.SemaphoreType.DMA((CHUNKS, n)),
        ],
        compiler_params=pltpu.CompilerParams(
            collective_id=1, has_side_effects=True, vmem_limit_bytes=60 * 2**20
        ),
        name="tail",
    )(heads_rows, states, out_weight, up_weight, down_weight)
    return result.reshape(count, width)


def to_patches(cache, devices):
    frames, patch_count, width = cache.shape
    blocks = cache.reshape(frames, devices, patch_count // devices, width).transpose(1, 2, 0, 3)
    return lax.all_to_all(blocks, "tm", split_axis=0, concat_axis=0)


def body(
    n, devices,
    states, key_cache, value_cache, frame_times, valid_counts,
    qkv_weight, out_weight, up_weight, down_weight,
):
    frames, patch_count, width = states.shape
    share = patch_count // devices
    joined_weight = qkv_weight.reshape(qkv_weight.shape[0], 3 * width)
    frame_rows = states.reshape(-1, width)
    full_rows = lax.all_gather(frame_rows, "mp", axis=1, tiled=True)
    cached_keys = to_patches(key_cache, devices)
    cached_values = to_patches(value_cache, devices)
    projected = jnp.dot(unit_rows(full_rows), joined_weight, preferred_element_type=jnp.float32)
    projected = projected.astype(jnp.bfloat16).reshape(frames, devices, share, 3 * width)
    owned = lax.all_to_all(projected.transpose(1, 0, 2, 3), "tm", split_axis=0, concat_axis=0)
    fresh = owned.reshape(devices * frames, share, 3 * width).transpose(1, 0, 2)
    heads_out = attend(fresh, cached_keys, cached_values, frame_times, valid_counts)
    heads_out = heads_out.transpose(1, 0, 2).reshape(devices, frames, share, width)
    returned = lax.all_to_all(heads_out, "tm", split_axis=0, concat_axis=0)
    heads_rows = returned.transpose(1, 0, 2, 3).reshape(-1, width)
    result = tail(n, frame_rows, heads_rows, out_weight, up_weight, down_weight)
    return result.reshape(states.shape)


def solution(mesh):
    in_specs = (
        P("tm", None, "mp"),
        P("tm", None, "mp"),
        P("tm", None, "mp"),
        P(),
        P("tm"),
        P(None, None, "mp"),
        P("mp", None),
        P(None, "mp"),
        P("mp", None),
    )
    out_specs = P("tm", None, "mp")
    run = functools.partial(body, mesh.shape["mp"], mesh.shape["tm"])
    return jax.shard_map(run, mesh=mesh, in_specs=in_specs, out_specs=out_specs, check_vma=False)
```

```python
import functools
import math

import jax
import jax.numpy as jnp
from jax import lax
from jax.experimental import pallas as pl
from jax.experimental.pallas import tpu as pltpu
from jax.sharding import PartitionSpec as P

HD = 128
GROUP = 8
MESH = pl.DeviceIdType.MESH


def unit_rows(tensor):
    widened = tensor.astype(jnp.float32)
    mean_square = jnp.mean(widened * widened, axis=-1, keepdims=True)
    return (widened * lax.rsqrt(mean_square + 1e-06)).astype(jnp.bfloat16)


def block_kernel(
    n, peers, chunks, slab,
    states_hbm, keys_hbm, values_hbm, mask_ref, qkv_hbm, out_w_hbm, up_w_hbm, down_w_hbm,
    result_ref, keys_land, values_land,
    qkv_w, out_w, up_w, down_w, keys, values, fresh, returned, terms, landed, middle,
    local_sem, qkv_sem, own_sem, cache_send, cache_recv, fresh_send, fresh_recv, heads_send, heads_recv,
    sum_send, sum_recv, right_send, left_send, gather_recv,
):
    me = lax.axis_index("mp")
    here = lax.axis_index("tm")
    rows, width = returned.shape[1:]
    last = n - 1
    at_qkv = last
    at_attend = last + 1
    at_out = last + 2
    at_ffn = at_out + 2 * last

    def peer(k):
        return lax.rem(here + k, peers)

    states_load = pltpu.make_async_copy(states_hbm, middle.at[:, me], local_sem.at[0])
    states_load.start()
    caches = ((0, keys_hbm, keys_land, keys), (1, values_hbm, values_land, values))
    weight_loads = [
        pltpu.make_async_copy(src, dst, local_sem.at[k])
        for k, src, dst in ((1, out_w_hbm, out_w), (2, up_w_hbm, up_w), (3, down_w_hbm, down_w))
    ]

    def qkv_load(j, slot):
        return pltpu.make_async_copy(qkv_hbm.at[j], qkv_w.at[slot], qkv_sem.at[slot])

    qkv_load(0, 0).start()
    qkv_load(1, 1).start()

    barrier = pltpu.get_barrier_semaphore()
    for k in range(1, peers):
        pl.semaphore_signal(barrier, inc=1, device_id={"tm": peer(k)}, device_id_type=MESH)

    @pl.when(me > 0)
    def _():
        pl.semaphore_signal(barrier, inc=1, device_id={"mp": me - 1}, device_id_type=MESH)

    @pl.when(me < last)
    def _():
        pl.semaphore_signal(barrier, inc=1, device_id={"mp": me + 1}, device_id_type=MESH)

    @pl.when((me > 0) & (me < last))
    def _():
        pl.semaphore_wait(barrier, peers + 1)

    @pl.when((me == 0) | (me == last))
    def _():
        pl.semaphore_wait(barrier, peers)

    def cache_copy(kind, src, land, c, to, origin):
        return pltpu.make_async_remote_copy(
            src_ref=src.at[:, to * chunks + c],
            dst_ref=land.at[c, origin],
            send_sem=cache_send.at[c, kind, to],
            recv_sem=cache_recv.at[c, kind, origin],
            device_id={"tm": to},
            device_id_type=MESH,
        )

    def own_cache(kind, src, land, c):
        return pltpu.make_async_copy(
            src.at[:, here * chunks + c], land.at[c, here], own_sem.at[c, kind]
        )

    def send_cache(c):
        for kind, src, land, _ in caches:
            for k in range(1, peers):
                cache_copy(kind, src, land, c, peer(k), here).start()
            own_cache(kind, src, land, c).start()

    def slab_of(device):
        return pl.ds(pl.multiple_of(device * slab, slab), slab)

    def fresh_copy(c, to, origin):
        return pltpu.make_async_remote_copy(
            src_ref=terms.at[c, pl.ds(0, 3), slab_of(to)],
            dst_ref=fresh.at[c, :, slab_of(origin)],
            send_sem=fresh_send.at[c, to],
            recv_sem=fresh_recv.at[c, origin],
            device_id={"tm": to},
            device_id_type=MESH,
        )

    def own_fresh(c):
        return pltpu.make_async_copy(
            terms.at[c, pl.ds(0, 3), slab_of(here)], fresh.at[c, :, slab_of(here)], own_sem.at[c, 2]
        )

    def heads_copy(c, to, origin):
        return pltpu.make_async_remote_copy(
            src_ref=terms.at[c, last, slab_of(to)],
            dst_ref=returned.at[c, slab_of(origin)],
            send_sem=heads_send.at[c, to],
            recv_sem=heads_recv.at[c, origin],
            device_id={"tm": to},
            device_id_type=MESH,
        )

    def own_heads(c):
        return pltpu.make_async_copy(
            terms.at[c, last, slab_of(here)], returned.at[c, slab_of(here)], own_sem.at[c, 3]
        )

    def sum_copy(c, d, slot, target):
        return pltpu.make_async_remote_copy(
            src_ref=terms.at[c, d],
            dst_ref=landed.at[c, slot],
            send_sem=sum_send.at[c, d],
            recv_sem=sum_recv.at[c, slot],
            device_id={"mp": target},
            device_id_type=MESH,
        )

    def gather_copy(c, d, send_sem, target):
        return pltpu.make_async_remote_copy(
            src_ref=middle.at[c, d],
            dst_ref=middle.at[c, d],
            send_sem=send_sem.at[c, d],
            recv_sem=gather_recv.at[c, d],
            device_id={"mp": target},
            device_id_type=MESH,
        )

    def active(c):
        return (c >= 0) & (c < chunks)

    def add_landed(c, d, slot):
        sum_copy(c, d, slot, me).wait_recv()
        terms[c, d] = (
            terms[c, d].astype(jnp.float32) + landed[c, slot].astype(jnp.float32)
        ).astype(jnp.bfloat16)

    def sum_right(tick):
        c = tick - me
        for d in range(last, 0, -1):
            @pl.when(active(c) & (me < d))
            def _():
                @pl.when(me > 0)
                def _():
                    add_landed(c, d, d)

                sum_copy(c, d, d, me + 1).start()

    def sum_left(tick):
        c = tick - (last - me)
        for d in range(last):
            @pl.when(active(c) & (me > d))
            def _():
                @pl.when(me < last)
                def _():
                    add_landed(c, d, d)

                @pl.when(me - 1 == d)
                def _():
                    sum_copy(c, d, n, me - 1).start()

                @pl.when(me - 1 > d)
                def _():
                    sum_copy(c, d, d, me - 1).start()

    def wait_gather_sends(c):
        for d in range(n):
            @pl.when((d <= me) & (me < last))
            def _():
                gather_copy(c, d, right_send, me).wait_send()

            @pl.when((d >= me) & (me > 0))
            def _():
                gather_copy(c, d, left_send, me).wait_send()

    def gather_own(c):
        @pl.when(me < last)
        def _():
            gather_copy(c, me, right_send, me + 1).start()

        @pl.when(me > 0)
        def _():
            gather_copy(c, me, left_send, me - 1).start()

    def gather_hops(tick):
        for h in range(last, 0, -1):
            c = tick - h

            @pl.when(active(c) & (me - h >= 0))
            def _():
                gather_copy(c, me - h, right_send, me).wait_recv()

                @pl.when(me < last)
                def _():
                    gather_copy(c, me - h, right_send, me + 1).start()

            @pl.when(active(c) & (me + h <= last))
            def _():
                gather_copy(c, me + h, left_send, me).wait_recv()

                @pl.when(me > 0)
                def _():
                    gather_copy(c, me + h, left_send, me - 1).start()

    def normed_blocks(c):
        squares = jnp.zeros((rows, 1), jnp.float32)
        for d in range(n):
            block = middle[c, d].astype(jnp.float32)
            squares = squares + jnp.sum(block * block, axis=-1, keepdims=True)
        factor = lax.rsqrt(squares / (n * width) + 1e-06)
        return [(middle[c, d].astype(jnp.float32) * factor).astype(jnp.bfloat16) for d in range(n)]

    def product(blocks, weight):
        total = None
        for d in range(n):
            part = jnp.dot(
                blocks[d], weight[d * width : (d + 1) * width, :], preferred_element_type=jnp.float32
            )
            total = part if total is None else total + part
        return total

    def sum_end(c):
        @pl.when(me > 0)
        def _():
            sum_copy(c, me, me, me).wait_recv()

        @pl.when(me < last)
        def _():
            sum_copy(c, me, n, me).wait_recv()

        zero = jnp.zeros((rows, width), jnp.float32)
        from_left = jnp.where(me > 0, landed[c, me].astype(jnp.float32), zero)
        from_right = jnp.where(me < last, landed[c, n].astype(jnp.float32), zero)
        return terms[c, me].astype(jnp.float32) + from_left + from_right

    def wait_sum_sends(c):
        for d in range(n):
            @pl.when(me != d)
            def _():
                sum_copy(c, d, d, me).wait_send()

    def project(c):
        blocks = normed_blocks(c)
        for j in range(3):
            slot = lax.rem(c * 3 + j, 2)
            qkv_load(j, slot).wait()
            terms[c, j] = product(blocks, qkv_w.at[slot]).astype(jnp.bfloat16)

            @pl.when(c * 3 + j + 2 < 3 * chunks)
            def _():
                qkv_load((j + 2) % 3, slot).start()

        for k in range(1, peers):
            fresh_copy(c, peer(k), here).start()
        own_fresh(c).start()

    def attend(c):
        for kind, src, land, held in caches:
            for k in range(1, peers):
                cache_copy(kind, src, land, c, here, peer(k)).wait_recv()
            own_cache(kind, src, land, c).wait()
            pltpu.make_async_copy(land.at[c], held, local_sem.at[4 + kind]).start()
        for k in range(1, peers):
            fresh_copy(c, here, peer(k)).wait_recv()
        own_fresh(c).wait()
        for kind, _, land, held in caches:
            pltpu.make_async_copy(land.at[c], held, local_sem.at[4 + kind]).wait()
        mask = mask_ref[c].astype(jnp.float32)
        scale = 1.0 / math.sqrt(HD)
        for h in range(width // HD):
            at = slice(h * HD, (h + 1) * HD)
            old_keys = keys[:, :, :, at].astype(jnp.float32).reshape(-1, HD)
            old_values = values[:, :, :, at].astype(jnp.float32).reshape(-1, HD).astype(jnp.bfloat16)
            all_keys = jnp.concatenate([unit_rows(old_keys), unit_rows(fresh[c, 1, :, at])], axis=0)
            all_values = jnp.concatenate([old_values, fresh[c, 2, :, at]], axis=0)
            scores = lax.dot_general(
                unit_rows(fresh[c, 0, :, at]), all_keys, (((1,), (1,)), ((), ())),
                preferred_element_type=jnp.float32,
            )
            raised = jnp.exp(scores * scale) * mask
            weights = (raised / jnp.sum(raised, axis=-1, keepdims=True)).astype(jnp.bfloat16)
            terms[c, last, :, at] = jnp.dot(
                weights, all_values, preferred_element_type=jnp.float32
            ).astype(jnp.bfloat16)
        for k in range(1, peers):
            heads_copy(c, peer(k), here).start()
        own_heads(c).start()

    def project_out(c):
        for k in range(1, peers):
            heads_copy(c, here, peer(k)).wait_recv()
            heads_copy(c, peer(k), here).wait_send()
            fresh_copy(c, peer(k), here).wait_send()
        own_heads(c).wait()
        wait_gather_sends(c)
        block = returned[c]
        for d in range(n):
            terms[c, d] = jnp.dot(
                block, out_w[:, d * width : (d + 1) * width], preferred_element_type=jnp.float32
            ).astype(jnp.bfloat16)

    def feed_forward(c):
        wait_sum_sends(c)
        hidden = jax.nn.gelu(product(normed_blocks(c), up_w)).astype(jnp.bfloat16)
        for d in range(n):
            terms[c, d] = jnp.dot(
                hidden, down_w[:, d * width : (d + 1) * width], preferred_element_type=jnp.float32
            ).astype(jnp.bfloat16)

    def step(tick, carry):
        @pl.when((tick >= 2) & (tick < chunks))
        def _():
            send_cache(tick)

        @pl.when(tick < chunks)
        def _():
            gather_own(tick)

        gather_hops(tick)

        @pl.when(active(tick - at_qkv))
        def _():
            project(tick - at_qkv)

        gather_hops(tick - at_out - last)

        @pl.when(tick == at_out)
        def _():
            weight_loads[0].wait()

        @pl.when(active(tick - at_out))
        def _():
            project_out(tick - at_out)

        sum_right(tick - at_out)
        sum_left(tick - at_out)
        c_mid = tick - at_out - last

        @pl.when(active(c_mid))
        def _():
            total = sum_end(c_mid)
            middle[c_mid, me] = (middle[c_mid, me].astype(jnp.float32) + total).astype(jnp.bfloat16)
            gather_own(c_mid)

        @pl.when(tick == at_ffn)
        def _():
            weight_loads[1].wait()
            weight_loads[2].wait()

        @pl.when(active(tick - at_ffn))
        def _():
            feed_forward(tick - at_ffn)

        sum_right(tick - at_ffn)
        sum_left(tick - at_ffn)
        c_end = tick - at_ffn - last

        @pl.when(active(c_end))
        def _():
            total = sum_end(c_end)
            result_ref[c_end] = (middle[c_end, me].astype(jnp.float32) + total).astype(jnp.bfloat16)

        @pl.when(active(tick - at_attend))
        def _():
            attend(tick - at_attend)

        return carry

    states_load.wait()
    for c in range(min(2, chunks)):
        send_cache(c)
    for load in weight_loads:
        load.start()
    lax.fori_loop(0, chunks + at_ffn + last, step, 0)

    def drain(c, carry):
        wait_sum_sends(c)
        wait_gather_sends(c)
        for kind, src, land, _ in caches:
            for k in range(1, peers):
                cache_copy(kind, src, land, c, peer(k), here).wait_send()
        return carry

    lax.fori_loop(0, chunks, drain, 0)


def body(
    n, peers,
    states, key_cache, value_cache, frame_times, valid_counts,
    qkv_weight, out_weight, up_weight, down_weight,
):
    frames, patch_count, width = states.shape
    share = key_cache.shape[0]
    cache = share * peers
    chunks = patch_count // peers // GROUP
    slab = frames * GROUP
    rows = peers * slab

    row = jnp.arange(rows, dtype=jnp.int32)
    row_patch, row_frame = row % GROUP, row // GROUP
    column = jnp.arange(cache * GROUP, dtype=jnp.int32)
    column_patch, column_frame = column % GROUP, column // GROUP
    limits = (cache - valid_counts.reshape(chunks, GROUP))[:, row_patch]
    cached_ok = (row_patch[:, None] == column_patch[None, :])[None] & (
        column_frame[None, None, :] >= limits[:, :, None]
    )
    times = frame_times[row_frame]
    fresh_ok = (row_patch[:, None] == row_patch[None, :]) & (times[None, :] <= times[:, None])
    fresh_ok = jnp.broadcast_to(fresh_ok[None], (chunks, rows, rows))
    mask = jnp.concatenate([cached_ok, fresh_ok], axis=2).astype(jnp.bfloat16)

    arranged = states.reshape(frames, peers, chunks, GROUP, width).transpose(2, 1, 0, 3, 4)
    arranged = arranged.reshape(chunks, rows, width)
    keys = key_cache.reshape(share, peers * chunks, GROUP, width)
    values = value_cache.reshape(share, peers * chunks, GROUP, width)
    qkv = qkv_weight.transpose(1, 0, 2)

    vmem = pl.BlockSpec(memory_space=pltpu.VMEM)
    hbm = pl.BlockSpec(memory_space=pl.ANY)
    land = jax.ShapeDtypeStruct((chunks, peers, share, GROUP, width), jnp.bfloat16)
    bf16 = jnp.bfloat16
    dma = pltpu.SemaphoreType.DMA
    result, _, _ = pl.pallas_call(
        functools.partial(block_kernel, n, peers, chunks, slab),
        out_shape=(jax.ShapeDtypeStruct(arranged.shape, bf16), land, land),
        in_specs=[hbm, hbm, hbm, vmem, hbm, hbm, hbm, hbm],
        out_specs=(vmem, hbm, hbm),
        scratch_shapes=[
            pltpu.VMEM((2,) + qkv.shape[1:], bf16),
            pltpu.VMEM(out_weight.shape, bf16),
            pltpu.VMEM(up_weight.shape, bf16),
            pltpu.VMEM(down_weight.shape, bf16),
            pltpu.VMEM(land.shape[1:], bf16),
            pltpu.VMEM(land.shape[1:], bf16),
            pltpu.VMEM((chunks, 3, rows, width), bf16),
            pltpu.VMEM((chunks, rows, width), bf16),
            pltpu.VMEM((chunks, n, rows, width), bf16),
            pltpu.VMEM((chunks, n + 1, rows, width), bf16),
            pltpu.VMEM((chunks, n, rows, width), bf16),
            dma((6,)),
            dma((2,)),
            dma((chunks, 4)),
            dma((chunks, 2, peers)),
            dma((chunks, 2, peers)),
            dma((chunks, peers)),
            dma((chunks, peers)),
            dma((chunks, peers)),
            dma((chunks, peers)),
            dma((chunks, n)),
            dma((chunks, n + 1)),
            dma((chunks, n)),
            dma((chunks, n)),
            dma((chunks, n)),
        ],
        compiler_params=pltpu.CompilerParams(
            collective_id=1, has_side_effects=True, vmem_limit_bytes=62 * 2**20
        ),
        name="block",
    )(arranged, keys, values, mask, qkv, out_weight, up_weight, down_weight)
    result = result.reshape(chunks, peers, frames, GROUP, width).transpose(2, 1, 0, 3, 4)
    return result.reshape(states.shape)


def solution(mesh):
    in_specs = (
        P("tm", None, "mp"),
        P("tm", None, "mp"),
        P("tm", None, "mp"),
        P(),
        P("tm"),
        P(None, None, "mp"),
        P("mp", None),
        P(None, "mp"),
        P("mp", None),
    )
    out_specs = P("tm", None, "mp")
    run = functools.partial(body, mesh.shape["mp"], mesh.shape["tm"])
    return jax.shard_map(run, mesh=mesh, in_specs=in_specs, out_specs=out_specs, check_vma=False)
```

```python
import functools
import math

import jax
import jax.numpy as jnp
from jax import lax
from jax.experimental import pallas as pl
from jax.experimental.pallas import tpu as pltpu
from jax.sharding import PartitionSpec as P

HD = 128
GROUP = 8
MESH = pl.DeviceIdType.MESH


def unit_rows(tensor):
    widened = tensor.astype(jnp.float32)
    mean_square = jnp.mean(widened * widened, axis=-1, keepdims=True)
    return (widened * lax.rsqrt(mean_square + 1e-06)).astype(jnp.bfloat16)


def block_kernel(
    n, peers, chunks, slab,
    states_hbm, keys_hbm, values_hbm, mask_ref, qkv_hbm, out_w_hbm, up_w_hbm, down_w_hbm,
    result_ref, keys_land, values_land,
    qkv_w, out_w, up_w, down_w, keys, values, fresh, returned, terms, landed, middle,
    local_sem, qkv_sem, own_sem, cache_send, cache_recv, fresh_send, fresh_recv, heads_send, heads_recv,
    sum_send, sum_recv, right_send, left_send, gather_recv,
):
    me = lax.axis_index("mp")
    here = lax.axis_index("tm")
    rows, width = returned.shape[1:]
    last = n - 1
    at_qkv = last
    at_attend = last + 1
    at_out = last + 2
    at_ffn = at_out + 2 * last

    def peer(k):
        return lax.rem(here + k, peers)

    states_load = pltpu.make_async_copy(states_hbm, middle.at[:, me], local_sem.at[0])
    states_load.start()
    caches = ((0, keys_hbm, keys_land, keys), (1, values_hbm, values_land, values))
    weight_loads = [
        pltpu.make_async_copy(src, dst, local_sem.at[k])
        for k, src, dst in ((1, out_w_hbm, out_w), (2, up_w_hbm, up_w), (3, down_w_hbm, down_w))
    ]

    def qkv_load(j, slot):
        return pltpu.make_async_copy(qkv_hbm.at[j], qkv_w.at[slot], qkv_sem.at[slot])

    qkv_load(0, 0).start()
    qkv_load(1, 1).start()

    barrier = pltpu.get_barrier_semaphore()
    for k in range(1, peers):
        pl.semaphore_signal(barrier, inc=1, device_id={"tm": peer(k)}, device_id_type=MESH)

    @pl.when(me > 0)
    def _():
        pl.semaphore_signal(barrier, inc=1, device_id={"mp": me - 1}, device_id_type=MESH)

    @pl.when(me < last)
    def _():
        pl.semaphore_signal(barrier, inc=1, device_id={"mp": me + 1}, device_id_type=MESH)

    @pl.when((me > 0) & (me < last))
    def _():
        pl.semaphore_wait(barrier, peers + 1)

    @pl.when((me == 0) | (me == last))
    def _():
        pl.semaphore_wait(barrier, peers)

    def cache_copy(kind, src, land, c, to, origin):
        return pltpu.make_async_remote_copy(
            src_ref=src.at[:, to * chunks + c],
            dst_ref=land.at[c, origin],
            send_sem=cache_send.at[c, kind, to],
            recv_sem=cache_recv.at[c, kind, origin],
            device_id={"tm": to},
            device_id_type=MESH,
        )

    def own_cache(kind, src, land, c):
        return pltpu.make_async_copy(
            src.at[:, here * chunks + c], land.at[c, here], own_sem.at[c, kind]
        )

    def send_cache(c):
        for kind, src, land, _ in caches:
            for k in range(1, peers):
                cache_copy(kind, src, land, c, peer(k), here).start()
            own_cache(kind, src, land, c).start()

    def slab_of(device):
        return pl.ds(pl.multiple_of(device * slab, slab), slab)

    def fresh_copy(c, to, origin):
        return pltpu.make_async_remote_copy(
            src_ref=terms.at[c, pl.ds(0, 3), slab_of(to)],
            dst_ref=fresh.at[c, :, slab_of(origin)],
            send_sem=fresh_send.at[c, to],
            recv_sem=fresh_recv.at[c, origin],
            device_id={"tm": to},
            device_id_type=MESH,
        )

    def own_fresh(c):
        return pltpu.make_async_copy(
            terms.at[c, pl.ds(0, 3), slab_of(here)], fresh.at[c, :, slab_of(here)], own_sem.at[c, 2]
        )

    def heads_copy(c, to, origin):
        return pltpu.make_async_remote_copy(
            src_ref=terms.at[c, last, slab_of(to)],
            dst_ref=returned.at[c, slab_of(origin)],
            send_sem=heads_send.at[c, to],
            recv_sem=heads_recv.at[c, origin],
            device_id={"tm": to},
            device_id_type=MESH,
        )

    def own_heads(c):
        return pltpu.make_async_copy(
            terms.at[c, last, slab_of(here)], returned.at[c, slab_of(here)], own_sem.at[c, 3]
        )

    def sum_copy(c, d, slot, target):
        return pltpu.make_async_remote_copy(
            src_ref=terms.at[c, d],
            dst_ref=landed.at[c, slot],
            send_sem=sum_send.at[c, d],
            recv_sem=sum_recv.at[c, slot],
            device_id={"mp": target},
            device_id_type=MESH,
        )

    def gather_copy(c, d, send_sem, target):
        return pltpu.make_async_remote_copy(
            src_ref=middle.at[c, d],
            dst_ref=middle.at[c, d],
            send_sem=send_sem.at[c, d],
            recv_sem=gather_recv.at[c, d],
            device_id={"mp": target},
            device_id_type=MESH,
        )

    def active(c):
        return (c >= 0) & (c < chunks)

    def add_landed(c, d, slot):
        sum_copy(c, d, slot, me).wait_recv()
        terms[c, d] = (
            terms[c, d].astype(jnp.float32) + landed[c, slot].astype(jnp.float32)
        ).astype(jnp.bfloat16)

    def sum_right(tick):
        c = tick - me
        for d in range(last, 0, -1):
            @pl.when(active(c) & (me < d))
            def _():
                @pl.when(me > 0)
                def _():
                    add_landed(c, d, d)

                sum_copy(c, d, d, me + 1).start()

    def sum_left(tick):
        c = tick - (last - me)
        for d in range(last):
            @pl.when(active(c) & (me > d))
            def _():
                @pl.when(me < last)
                def _():
                    add_landed(c, d, d)

                @pl.when(me - 1 == d)
                def _():
                    sum_copy(c, d, n, me - 1).start()

                @pl.when(me - 1 > d)
                def _():
                    sum_copy(c, d, d, me - 1).start()

    def wait_gather_sends(c):
        for d in range(n):
            @pl.when((d <= me) & (me < last))
            def _():
                gather_copy(c, d, right_send, me).wait_send()

            @pl.when((d >= me) & (me > 0))
            def _():
                gather_copy(c, d, left_send, me).wait_send()

    def gather_own(c):
        @pl.when(me < last)
        def _():
            gather_copy(c, me, right_send, me + 1).start()

        @pl.when(me > 0)
        def _():
            gather_copy(c, me, left_send, me - 1).start()

    def gather_hops(tick):
        for h in range(last, 0, -1):
            c = tick - h

            @pl.when(active(c) & (me - h >= 0))
            def _():
                gather_copy(c, me - h, right_send, me).wait_recv()

                @pl.when(me < last)
                def _():
                    gather_copy(c, me - h, right_send, me + 1).start()

            @pl.when(active(c) & (me + h <= last))
            def _():
                gather_copy(c, me + h, left_send, me).wait_recv()

                @pl.when(me > 0)
                def _():
                    gather_copy(c, me + h, left_send, me - 1).start()

    def normed_blocks(c):
        squares = jnp.zeros((rows, 1), jnp.float32)
        for d in range(n):
            block = middle[c, d].astype(jnp.float32)
            squares = squares + jnp.sum(block * block, axis=-1, keepdims=True)
        factor = lax.rsqrt(squares / (n * width) + 1e-06)
        return [(middle[c, d].astype(jnp.float32) * factor).astype(jnp.bfloat16) for d in range(n)]

    def product(blocks, weight):
        total = None
        for d in range(n):
            part = jnp.dot(
                blocks[d], weight[d * width : (d + 1) * width, :], preferred_element_type=jnp.float32
            )
            total = part if total is None else total + part
        return total

    def sum_end(c):
        @pl.when(me > 0)
        def _():
            sum_copy(c, me, me, me).wait_recv()

        @pl.when(me < last)
        def _():
            sum_copy(c, me, n, me).wait_recv()

        zero = jnp.zeros((rows, width), jnp.float32)
        from_left = jnp.where(me > 0, landed[c, me].astype(jnp.float32), zero)
        from_right = jnp.where(me < last, landed[c, n].astype(jnp.float32), zero)
        return terms[c, me].astype(jnp.float32) + from_left + from_right

    def wait_sum_sends(c):
        for d in range(n):
            @pl.when(me != d)
            def _():
                sum_copy(c, d, d, me).wait_send()

    def project(c):
        blocks = normed_blocks(c)
        for j in range(3):
            slot = lax.rem(c * 3 + j, 2)
            qkv_load(j, slot).wait()
            terms[c, j] = product(blocks, qkv_w.at[slot]).astype(jnp.bfloat16)

            @pl.when(c * 3 + j + 2 < 3 * chunks)
            def _():
                qkv_load((j + 2) % 3, slot).start()

        for k in range(1, peers):
            fresh_copy(c, peer(k), here).start()
        own_fresh(c).start()

    def attend(c):
        for kind, src, land, held in caches:
            for k in range(1, peers):
                cache_copy(kind, src, land, c, here, peer(k)).wait_recv()
            own_cache(kind, src, land, c).wait()
            pltpu.make_async_copy(land.at[c], held, local_sem.at[4 + kind]).start()
        for k in range(1, peers):
            fresh_copy(c, here, peer(k)).wait_recv()
        own_fresh(c).wait()
        for kind, _, land, held in caches:
            pltpu.make_async_copy(land.at[c], held, local_sem.at[4 + kind]).wait()
        mask = mask_ref[c].astype(jnp.float32)
        scale = 1.0 / math.sqrt(HD)
        for h in range(width // HD):
            at = slice(h * HD, (h + 1) * HD)
            old_keys = keys[:, :, :, at].astype(jnp.float32).reshape(-1, HD)
            old_values = values[:, :, :, at].astype(jnp.float32).reshape(-1, HD).astype(jnp.bfloat16)
            all_keys = jnp.concatenate([unit_rows(old_keys), unit_rows(fresh[c, 1, :, at])], axis=0)
            all_values = jnp.concatenate([old_values, fresh[c, 2, :, at]], axis=0)
            scores = lax.dot_general(
                unit_rows(fresh[c, 0, :, at]), all_keys, (((1,), (1,)), ((), ())),
                preferred_element_type=jnp.float32,
            )
            raised = jnp.exp(scores * scale) * mask
            weights = (raised / jnp.sum(raised, axis=-1, keepdims=True)).astype(jnp.bfloat16)
            terms[c, last, :, at] = jnp.dot(
                weights, all_values, preferred_element_type=jnp.float32
            ).astype(jnp.bfloat16)
        for k in range(1, peers):
            heads_copy(c, peer(k), here).start()
        own_heads(c).start()

    def project_out(c):
        for k in range(1, peers):
            heads_copy(c, here, peer(k)).wait_recv()
            heads_copy(c, peer(k), here).wait_send()
            fresh_copy(c, peer(k), here).wait_send()
        own_heads(c).wait()
        wait_gather_sends(c)
        block = returned[c]
        for d in range(n):
            terms[c, d] = jnp.dot(
                block, out_w[:, d * width : (d + 1) * width], preferred_element_type=jnp.float32
            ).astype(jnp.bfloat16)

    def feed_forward(c):
        wait_sum_sends(c)
        hidden = jax.nn.gelu(product(normed_blocks(c), up_w)).astype(jnp.bfloat16)
        for d in range(n):
            terms[c, d] = jnp.dot(
                hidden, down_w[:, d * width : (d + 1) * width], preferred_element_type=jnp.float32
            ).astype(jnp.bfloat16)

    def step(tick, carry):
        @pl.when((tick >= 2) & (tick < chunks))
        def _():
            send_cache(tick)

        @pl.when(tick < chunks)
        def _():
            gather_own(tick)

        gather_hops(tick)

        @pl.when(active(tick - at_qkv))
        def _():
            project(tick - at_qkv)

        gather_hops(tick - at_out - last)

        @pl.when(tick == at_out)
        def _():
            weight_loads[0].wait()

        @pl.when(active(tick - at_out))
        def _():
            project_out(tick - at_out)

        sum_right(tick - at_out)
        sum_left(tick - at_out)
        c_mid = tick - at_out - last

        @pl.when(active(c_mid))
        def _():
            total = sum_end(c_mid)
            middle[c_mid, me] = (middle[c_mid, me].astype(jnp.float32) + total).astype(jnp.bfloat16)
            gather_own(c_mid)

        @pl.when(tick == at_ffn)
        def _():
            weight_loads[1].wait()
            weight_loads[2].wait()

        @pl.when(active(tick - at_ffn))
        def _():
            feed_forward(tick - at_ffn)

        sum_right(tick - at_ffn)
        sum_left(tick - at_ffn)
        c_end = tick - at_ffn - last

        @pl.when(active(c_end))
        def _():
            total = sum_end(c_end)
            result_ref[c_end] = (middle[c_end, me].astype(jnp.float32) + total).astype(jnp.bfloat16)

        @pl.when(active(tick - at_attend))
        def _():
            attend(tick - at_attend)

        return carry

    states_load.wait()
    for c in range(min(2, chunks)):
        send_cache(c)
    for load in weight_loads:
        load.start()
    lax.fori_loop(0, chunks + at_ffn + last, step, 0)

    def drain(c, carry):
        wait_sum_sends(c)
        wait_gather_sends(c)
        for kind, src, land, _ in caches:
            for k in range(1, peers):
                cache_copy(kind, src, land, c, peer(k), here).wait_send()
        return carry

    lax.fori_loop(0, chunks, drain, 0)


def body(
    n, peers,
    states, key_cache, value_cache, frame_times, valid_counts,
    qkv_weight, out_weight, up_weight, down_weight,
):
    frames, patch_count, width = states.shape
    share = key_cache.shape[0]
    cache = share * peers
    chunks = patch_count // peers // GROUP
    slab = frames * GROUP
    rows = peers * slab

    row = jnp.arange(rows, dtype=jnp.int32)
    row_patch = row % GROUP
    column = jnp.arange(cache * GROUP, dtype=jnp.int32)
    column_patch, column_frame = column % GROUP, column // GROUP
    limits = cache - valid_counts.reshape(chunks, 1, GROUP)
    limits = jnp.broadcast_to(limits, (chunks, rows // GROUP, GROUP)).reshape(chunks, rows)
    cached_ok = (row_patch[:, None] == column_patch[None, :])[None] & (
        column_frame[None, None, :] >= limits[:, :, None]
    )
    times = jnp.broadcast_to(frame_times[:, None], (rows // GROUP, GROUP)).reshape(rows)
    fresh_ok = (row_patch[:, None] == row_patch[None, :]) & (times[None, :] <= times[:, None])
    fresh_ok = jnp.broadcast_to(fresh_ok[None], (chunks, rows, rows))
    mask = jnp.concatenate([cached_ok, fresh_ok], axis=2).astype(jnp.bfloat16)

    arranged = states.reshape(frames, peers, chunks, GROUP, width).transpose(2, 1, 0, 3, 4)
    arranged = arranged.reshape(chunks, rows, width)
    keys = key_cache.reshape(share, peers * chunks, GROUP, width)
    values = value_cache.reshape(share, peers * chunks, GROUP, width)
    qkv = qkv_weight.transpose(1, 0, 2)

    vmem = pl.BlockSpec(memory_space=pltpu.VMEM)
    hbm = pl.BlockSpec(memory_space=pl.ANY)
    land = jax.ShapeDtypeStruct((chunks, peers, share, GROUP, width), jnp.bfloat16)
    bf16 = jnp.bfloat16
    dma = pltpu.SemaphoreType.DMA
    result, _, _ = pl.pallas_call(
        functools.partial(block_kernel, n, peers, chunks, slab),
        out_shape=(jax.ShapeDtypeStruct(arranged.shape, bf16), land, land),
        in_specs=[hbm, hbm, hbm, vmem, hbm, hbm, hbm, hbm],
        out_specs=(vmem, hbm, hbm),
        scratch_shapes=[
            pltpu.VMEM((2,) + qkv.shape[1:], bf16),
            pltpu.VMEM(out_weight.shape, bf16),
            pltpu.VMEM(up_weight.shape, bf16),
            pltpu.VMEM(down_weight.shape, bf16),
            pltpu.VMEM(land.shape[1:], bf16),
            pltpu.VMEM(land.shape[1:], bf16),
            pltpu.VMEM((chunks, 3, rows, width), bf16),
            pltpu.VMEM((chunks, rows, width), bf16),
            pltpu.VMEM((chunks, n, rows, width), bf16),
            pltpu.VMEM((chunks, n + 1, rows, width), bf16),
            pltpu.VMEM((chunks, n, rows, width), bf16),
            dma((6,)),
            dma((2,)),
            dma((chunks, 4)),
            dma((chunks, 2, peers)),
            dma((chunks, 2, peers)),
            dma((chunks, peers)),
            dma((chunks, peers)),
            dma((chunks, peers)),
            dma((chunks, peers)),
            dma((chunks, n)),
            dma((chunks, n + 1)),
            dma((chunks, n)),
            dma((chunks, n)),
            dma((chunks, n)),
        ],
        compiler_params=pltpu.CompilerParams(
            collective_id=1, has_side_effects=True, vmem_limit_bytes=62 * 2**20
        ),
        name="block",
    )(arranged, keys, values, mask, qkv, out_weight, up_weight, down_weight)
    result = result.reshape(chunks, peers, frames, GROUP, width).transpose(2, 1, 0, 3, 4)
    return result.reshape(states.shape)


def solution(mesh):
    in_specs = (
        P("tm", None, "mp"),
        P("tm", None, "mp"),
        P("tm", None, "mp"),
        P(),
        P("tm"),
        P(None, None, "mp"),
        P("mp", None),
        P(None, "mp"),
        P("mp", None),
    )
    out_specs = P("tm", None, "mp")
    run = functools.partial(body, mesh.shape["mp"], mesh.shape["tm"])
    return jax.shard_map(run, mesh=mesh, in_specs=in_specs, out_specs=out_specs, check_vma=False)
```
